32 devices in a mesh: sweep: 2 (over x), row: 16 (over z, y, core).
Axes of the slice: x: 2, y: 2, z: 4, core: 2. Of those that a mesh axis runs over, the one named last changes fastest.
Arguments:
- alphas: float32 [4], P('sweep'), parts along dimension 0, may hold values from 0.75 to 0.95
- base_scores: float32 [172, 16384], P(None, 'row'), may hold values from 0 to 1
- tile_values: bfloat16 [2560, 128, 128], P('row')
- tile_rows: int32 [2560], P('row'), may hold values from 0 to 7
- tile_cols: int32 [2560], P('row'), may hold values from 0 to 8
- send_rows: int32 [16, 4, 32], P('row'), may hold values from 0 to 1023
- send_count: int32 [16, 4], P('row'), may hold values from 0 to 32, as said below
- train_nodes: int32 [1024], P('row'), may hold values from 0 to 1023, as said below
- train_labels: int32 [1024], P('row'), may hold values from 0 to 171
Outputs:
- smoothed: float32 [344, 16384], P('sweep', 'row'), parts along dimension 0
The draws below stay inside these ranges and needn't reach their ends.
There are 2 independent parts, one for each index of `sweep`. The reference program is written for one: setup_inputs(seed, part) draws one part's arguments, and reference() takes and returns one part's arrays. A program takes and returns all parts, laid end to end along the dimension named above; an argument that names none is the same for every part. Nothing has to cross between parts.
Inputs may be any that keep to these rules, and one draw needn't show every extreme that they name: `send_count`: zero where the receiving partition index lies outside the axis; in every draw one partition receives 32 live entries from each of its neighbours. `train_nodes`: distinct within each partition's block of 64 entries.
All inputs are finite; a program needn't handle non-finite values.
Results may differ from the reference program's by a relative error of at most 0.00093.
Values may be sent and summed in bfloat16 or wider, within the bound.
A program may use at most 128 MiB of HBM per device.

```python
import jax
import jax.numpy as jnp
from jax import lax

C = 172
TILE = 128
BLK_DEV = 8
TPB = 20
SEND_PEER = 32
REACH = 2
HOPS = 2
NODES_DEV = 1024
TILES_DEV = 160
TRAIN_DEV = 64
HALO = 128
NODES = 16384
TILES = 2560
TRAIN = 1024
N_ROW = 16


def draw_send_count(key, part):
    key = jax.random.fold_in(key, 7)
    slots = 2 * REACH
    counts = jax.random.randint(key, (N_ROW, slots), 1, SEND_PEER + 1)
    offset_table = jnp.array([value for value in range(-REACH, REACH + 1) if value != 0], jnp.int32)
    device_ids = jnp.arange(N_ROW, dtype=jnp.int32)[:, None]
    target = device_ids + offset_table[None, :]
    counts = jnp.where(target == N_ROW // 2, SEND_PEER, counts)
    counts = jnp.where((target >= 0) & (target < N_ROW), counts, 0)
    return counts.astype(jnp.int32)


def pick_nodes(node_key):
    return jax.random.permutation(node_key, NODES_DEV)[:TRAIN_DEV]


def draw_train_nodes(key, part):
    key = jax.random.fold_in(key, 11)
    keys = jax.random.split(key, N_ROW)
    picks = jax.vmap(pick_nodes)(keys)
    return picks.reshape(-1).astype(jnp.int32)


def draw_tile_values(key, part):
    key = jax.random.fold_in(key, 13)
    value_key, edge_key = jax.random.split(key)
    shape = (N_ROW, TILES_DEV, TILE, TILE)
    position = jnp.arange(N_ROW, dtype=jnp.float32) / (N_ROW - 1)
    logs = jax.random.uniform(value_key, shape, jnp.float32, jnp.log(0.25), jnp.log(1.75))
    entries = jnp.exp(logs) / 0.77
    rise = 0.5 * jnp.power(5.0, position)
    edge_draw = jax.random.uniform(edge_key, shape, jnp.float32)
    present = jnp.where(edge_draw < 0.01, 100.0, 0.0)
    scaled = entries * present * rise[:, None, None, None] / (TPB * TILE)
    return scaled.reshape(TILES, TILE, TILE).astype(jnp.bfloat16)


def plant(result, own_key, least, high):
    place = [jax.random.randint(jax.random.fold_in(own_key, axis), (), 0, length) for axis, length in enumerate(result.shape)]
    main_axis = result.shape.index(max(result.shape))
    beside = place[:main_axis] + [(place[main_axis] + 1) % result.shape[main_axis]] + place[main_axis + 1:]
    return result.at[tuple(place)].set(least).at[tuple(beside)].set(high)


def steps_of(key, extent, shards, least, top_value):
    loudness = 1.0
    for dim, blocks in shards:
        heights = jax.random.uniform(jax.random.fold_in(jax.random.fold_in(key, 6), dim), (blocks,), jnp.float32, least / len(shards), top_value / len(shards))
        loudness = loudness * jnp.repeat(jnp.exp(heights), extent[dim] // blocks).reshape((-1,) + (1,) * (len(extent) - 1 - dim))
    return loudness


def setup_inputs(seed: int = 0, part: int = 0) -> dict:
    key_list = jax.random.split(jax.random.key(seed), 10)
    part_keys = jax.random.split(jax.random.fold_in(key_list[9], part), 10)
    return {
        "alphas": jnp.clip(jax.random.uniform(part_keys[0], (2,), jnp.float32, 0.75, 0.95), 0.75, 0.95),
        "base_scores": jnp.clip(1.0 * jax.random.uniform(key_list[1], (C, NODES), jnp.float32) ** steps_of(key_list[1], (C, NODES), ((1, 16),), -0.2, 0.2), 0.0, 1.0),
        "tile_values": draw_tile_values(jax.random.fold_in(key_list[9], 71), part),
        "tile_rows": plant(jax.random.randint(key_list[3], (TILES,), 0, BLK_DEV), jax.random.fold_in(key_list[3], 1), 0, BLK_DEV - 1).astype(jnp.int32),
        "tile_cols": plant(jax.random.randint(key_list[4], (TILES,), 0, BLK_DEV + HALO // TILE), jax.random.fold_in(key_list[4], 1), 0, (BLK_DEV + HALO // TILE) - 1).astype(jnp.int32),
        "send_rows": plant(jax.random.randint(key_list[5], (N_ROW, 2 * REACH, SEND_PEER), 0, NODES_DEV), jax.random.fold_in(key_list[5], 1), 0, NODES_DEV - 1).astype(jnp.int32),
        "send_count": draw_send_count(jax.random.fold_in(key_list[9], 71), part),
        "train_nodes": draw_train_nodes(jax.random.fold_in(key_list[9], 71), part),
        "train_labels": plant(jax.random.randint(key_list[8], (TRAIN,), 0, C), jax.random.fold_in(key_list[8], 1), 0, C - 1).astype(jnp.int32),
    }


def slot_offsets():
    return [value for value in range(-REACH, REACH + 1) if value != 0]


def take_rows(device_values, device_rows):
    return device_values[:, device_rows]


def neighbour_halo(values, send_rows, send_count):
    slots = 2 * REACH
    picked = jax.vmap(take_rows)(values, send_rows)
    live_slots = jnp.arange(SEND_PEER)[None, None, :] < send_count[:, :, None]
    picked = jnp.where(live_slots[:, None, :, :], picked, jnp.zeros_like(picked))
    device_ids = jnp.arange(N_ROW)
    pieces = []
    for slot_index in range(slots):
        offset_value = slot_offsets()[slot_index]
        source = picked[:, :, slots - 1 - slot_index, :]
        rolled = jnp.roll(source, -offset_value, axis=0)
        inside = (device_ids + offset_value >= 0) & (device_ids + offset_value < N_ROW)
        pieces.append(jnp.where(inside[:, None, None], rolled, jnp.zeros_like(rolled)))
    halo_rows = jnp.stack(pieces, axis=2)
    return halo_rows.reshape(N_ROW, values.shape[1], slots * SEND_PEER)


def device_product(operands):
    extended, tile_block, row_list, col_list = operands
    blocks = extended.reshape(extended.shape[0], -1, TILE)
    gathered = blocks[:, col_list, :].astype(jnp.float32)
    products = jnp.einsum('ctv,tvu->ctu', gathered, tile_block.astype(jnp.float32), precision=lax.Precision.HIGHEST)
    selector = (row_list[:, None] == jnp.arange(BLK_DEV)[None, :]).astype(jnp.float32)
    summed = jnp.einsum('ctu,tr->cru', products, selector, precision=lax.Precision.HIGHEST)
    return summed.reshape(extended.shape[0], BLK_DEV * TILE)


def propagate(values, tile_values, tile_rows, tile_cols, send_rows, send_count):
    halo_rows = neighbour_halo(values, send_rows, send_count)
    extended = jnp.concatenate([values, halo_rows], axis=2)
    return lax.map(device_product, (extended, tile_values.reshape(N_ROW, TILES_DEV, TILE, TILE), tile_rows.reshape(N_ROW, TILES_DEV), tile_cols.reshape(N_ROW, TILES_DEV)))


def reference(alphas, base_scores, tile_values, tile_rows, tile_cols, send_rows, send_count, train_nodes, train_labels):
    scores = base_scores.reshape(C, N_ROW, NODES_DEV).transpose(1, 0, 2)
    node_lists = train_nodes.reshape(N_ROW, TRAIN_DEV)
    label_lists = train_labels.reshape(N_ROW, TRAIN_DEV)
    placed = (node_lists[:, :, None] == jnp.arange(NODES_DEV)[None, None, :]).astype(jnp.float32)
    onehot = (label_lists[:, :, None] == jnp.arange(C)[None, None, :]).astype(jnp.float32)
    truth = jnp.einsum('ntc,ntm->ncm', onehot, placed, precision=lax.Precision.HIGHEST)
    labelled = jnp.sum(placed, axis=1)[:, None, :]
    error_start = labelled * (truth - scores)
    errors = error_start
    for repeat in range(HOPS):
        spread_out = propagate(errors.astype(jnp.bfloat16), tile_values, tile_rows, tile_cols, send_rows, send_count)
        errors = (1.0 - alphas[0]) * error_start + alphas[0] * spread_out
    entries = TRAIN * C
    error_mass = jnp.sum(jnp.abs(error_start))
    spread_total = jnp.sum(labelled * jnp.abs(errors))
    autoscale = (error_mass / entries) / (spread_total / entries + 1e-6)
    corrected = scores + autoscale * errors
    anchored = labelled * truth + (1.0 - labelled) * corrected
    smoothed = anchored
    for repeat in range(HOPS):
        spread_out = propagate(smoothed.astype(jnp.bfloat16), tile_values, tile_rows, tile_cols, send_rows, send_count)
        smoothed = (1.0 - alphas[1]) * anchored + alphas[1] * spread_out
        smoothed = labelled * truth + (1.0 - labelled) * smoothed
    return smoothed.transpose(1, 0, 2).reshape(C, NODES)
```

```python
import functools

import jax
import jax.numpy as jnp
from jax import lax
from jax.experimental import pallas as pl
from jax.experimental.pallas import tpu as pltpu
from jax.sharding import PartitionSpec as P

CHUNKS = 8
MESH = pl.DeviceIdType.MESH
BF = jnp.bfloat16
F32 = jnp.float32


def dot(a, b):
    return jnp.dot(a, b, preferred_element_type=F32)


def dot_nt(a, b, precision=None):
    return lax.dot_general(a, b, (((1,), (1,)), ((), ())), precision=precision, preferred_element_type=F32)


def dot_tn(a, b):
    return lax.dot_general(a, b, (((0,), (0,)), ((), ())), preferred_element_type=F32)


def split(x):
    high = x.astype(BF)
    return high, (x - high.astype(F32)).astype(BF)


def dense_body(rows, cols, tiles, high, low, held, acc, sems):
    count, tile, _ = tiles.shape
    col_blocks, row_blocks = acc.shape[:2]
    step = count // CHUNKS
    copies = []
    for chunk in range(CHUNKS):
        part = pl.ds(chunk * step, step)
        copies.append(pltpu.make_async_copy(tiles.at[part], held.at[part], sems.at[chunk]))
        copies[-1].start()
    acc[...] = jnp.zeros_like(acc)
    for chunk in range(CHUNKS):
        copies[chunk].wait()

        def add(t, _):
            at = (cols[t], rows[t])
            acc[at] += held[t].astype(F32)
            return 0

        lax.fori_loop(chunk * step, (chunk + 1) * step, add, 0, unroll=4)
    for c in range(col_blocks):
        for r in range(row_blocks):
            high_part, low_part = split(acc[c, r])
            high[c * tile : (c + 1) * tile, r * tile : (r + 1) * tile] = high_part
            low[c * tile : (c + 1) * tile, r * tile : (r + 1) * tile] = low_part


def dense(tile_rows, tile_cols, tile_values, nodes, halo):
    count, tile, _ = tile_values.shape
    shape = jax.ShapeDtypeStruct((nodes + halo, nodes), BF)
    return pl.pallas_call(
        dense_body,
        out_shape=(shape, shape),
        in_specs=[
            pl.BlockSpec(memory_space=pltpu.SMEM),
            pl.BlockSpec(memory_space=pltpu.SMEM),
            pl.BlockSpec(memory_space=pl.ANY),
        ],
        out_specs=(pl.BlockSpec(memory_space=pltpu.VMEM),) * 2,
        scratch_shapes=[
            pltpu.VMEM((count, tile, tile), BF),
            pltpu.VMEM(((nodes + halo) // tile, nodes // tile, tile, tile), F32),
            pltpu.SemaphoreType.DMA((CHUNKS,)),
        ],
        compiler_params=pltpu.CompilerParams(vmem_limit_bytes=40 << 20),
        name="dense",
    )(tile_rows, tile_cols, tile_values)


def spread_body(
    n, alphas, counts, base, send_rows, nodes, labels, high_in, low_in, out,
    high, low, pick, start, fixed, truth, sent0, sent1, sent2, sent3, got0, got1, got2, got3,
    part, parts, send_sems, recv_sems, part_send, part_recv, load_sems,
):
    channels, local = base.shape
    slots, size = send_rows.shape[1:]
    reach = slots // 2
    offsets = [value for value in range(-reach, reach + 1) if value != 0]
    me = lax.axis_index("row")
    sent, got = (sent0, sent1, sent2, sent3), (got0, got1, got2, got3)

    barrier = pltpu.get_barrier_semaphore()

    def greet(k, _):
        pl.semaphore_signal(barrier, inc=1, device_id={"row": lax.rem(me + k, n)}, device_id_type=MESH)
        return 0

    lax.fori_loop(1, n, greet, 0)
    loads = [pltpu.make_async_copy(high_in, high, load_sems.at[0]), pltpu.make_async_copy(low_in, low, load_sems.at[1])]
    for load in loads:
        load.start()

    def inside(offset):
        return (me + offset >= 0) & (me + offset < n)

    for slot, offset in enumerate(offsets):

        @pl.when(jnp.logical_not(inside(offset)))
        def _():
            for buffer in got:
                buffer[slot] = jnp.zeros(buffer.shape[1:], BF)

    def copy(turn, k):
        return pltpu.make_async_remote_copy(
            src_ref=sent[turn].at[k],
            dst_ref=got[turn].at[slots - 1 - k],
            send_sem=send_sems.at[turn, k],
            recv_sem=recv_sems.at[turn, slots - 1 - k],
            device_id={"row": me + offsets[k]},
            device_id_type=MESH,
        )

    def send(turn, planes):
        picked = [dot_nt(pick[...], plane).astype(BF) for plane in planes]
        for k in range(slots):
            for at, plane in enumerate(picked):
                sent[turn][k, at * size : (at + 1) * size, :] = plane[k * size : (k + 1) * size, :]

    def launch(turn):
        for k, offset in enumerate(offsets):

            @pl.when(inside(offset))
            def _():
                copy(turn, k).start()

    def receive(turn):
        for slot, offset in enumerate(offsets):

            @pl.when(inside(offset))
            def _():
                copy(turn, slots - 1 - slot).wait_recv()

        planes = got[turn].shape[1] // size
        return [
            jnp.concatenate([got[turn][slot, at * size : (at + 1) * size, :] for slot in range(slots)], axis=0)
            for at in range(planes)
        ]

    def local_product(values):
        return dot(values, high[:local, :]) + dot(values, low[:local, :])

    def halo_product(values):
        return dot_tn(values, high[local:, :]) + dot_tn(values, low[local:, :])

    eye = jnp.where(
        lax.broadcasted_iota(jnp.int32, (size, size), 0) == lax.broadcasted_iota(jnp.int32, (size, size), 1), 1.0, 0.0
    ).astype(F32)
    wanted = dot_nt(eye, send_rows[0].astype(F32), precision=lax.Precision.HIGHEST).astype(jnp.int32)
    column = lax.broadcasted_iota(jnp.int32, (size, local), 1)
    place = lax.broadcasted_iota(jnp.int32, (size, local), 0)
    for k in range(slots):
        live = (column == wanted[:, k : k + 1]) & (place < counts[0, k])
        pick[k * size : (k + 1) * size, :] = jnp.where(live, 1.0, 0.0).astype(BF)

    count = nodes.shape[1]
    placed = jnp.where(lax.broadcasted_iota(jnp.int32, (local, count), 0) == nodes[...], 1.0, 0.0).astype(BF)
    onehot = jnp.where(lax.broadcasted_iota(jnp.int32, (channels, count), 0) == labels[...], 1.0, 0.0).astype(BF)
    truth[...] = dot_nt(onehot, placed)
    labelled = dot_nt(jnp.ones((8, count), BF), placed)[0:1, :]
    free = 1.0 - labelled
    start[...] = labelled * (truth[...] - base[...])
    fixed[...] = truth[...] + free * base[...]
    values = start[...].astype(BF)
    fixed_high, fixed_low = split(fixed[...])
    send(0, [values, fixed_high, fixed_low])
    pl.semaphore_wait(barrier, n - 1)
    launch(0)

    def folded(x):
        row = jnp.sum(x, axis=0, keepdims=True)
        return sum(row[:, at : at + 128] for at in range(0, local, 128))

    part[...] = jnp.zeros_like(part)
    part[0:1, :] = folded(jnp.abs(start[...]))

    weight = alphas[0]
    for load in loads:
        load.wait()
    total = local_product(values)
    total = total + halo_product(receive(0)[0])
    errors = (1.0 - weight) * start[...] + weight * total
    values = errors.astype(BF)
    send(1, [values])
    launch(1)
    total = local_product(values)
    total = total + halo_product(receive(1)[0])
    errors = (1.0 - weight) * start[...] + weight * total
    part[1:2, :] = folded(labelled * jnp.abs(errors))

    def part_copy(k):
        return pltpu.make_async_remote_copy(
            src_ref=part,
            dst_ref=parts.at[k - 1],
            send_sem=part_send.at[k - 1],
            recv_sem=part_recv.at[k - 1],
            device_id={"row": lax.rem(me + k, n)},
            device_id_type=MESH,
        )

    def part_start(k, _):
        part_copy(k).start()
        return 0

    lax.fori_loop(1, n, part_start, 0)
    moving = free * errors
    moving_high, moving_low = split(moving)
    send(2, [moving_high, moving_low])
    launch(2)

    def part_wait(k, _):
        part_copy(k).wait_recv()
        return 0

    lax.fori_loop(1, n, part_wait, 0)
    sums = part[...] + jnp.sum(parts[...], axis=0)
    entries = n * count * channels
    mass = jnp.sum(sums[0:1, :], axis=1, keepdims=True) / entries
    spread = jnp.sum(sums[1:2, :], axis=1, keepdims=True) / entries
    scale = mass / (spread + 1e-06)
    anchored = fixed[...] + scale * moving
    start[...] = anchored
    values = anchored.astype(BF)
    weight = alphas[1]
    total = local_product(values)
    fixed_high, fixed_low = [
        jnp.concatenate([got0[slot, at * size : (at + 1) * size, :] for slot in range(slots)], axis=0).astype(F32)
        for at in (1, 2)
    ]
    moving_high, moving_low = [plane.astype(F32) for plane in receive(2)]
    halo = (fixed_high + fixed_low) + scale * (moving_high + moving_low)
    total = total + halo_product(halo.astype(BF))
    smoothed = truth[...] + free * ((1.0 - weight) * start[...] + weight * total)
    values = smoothed.astype(BF)
    send(3, [values])
    launch(3)
    total = local_product(values)
    total = total + halo_product(receive(3)[0])
    out[...] = truth[...] + free * ((1.0 - weight) * start[...] + weight * total)

    for turn in range(4):
        for k, offset in enumerate(offsets):

            @pl.when(inside(offset))
            def _():
                copy(turn, k).wait_send()

    def part_end(k, _):
        part_copy(k).wait_send()
        return 0

    lax.fori_loop(1, n, part_end, 0)


def shards(
    alphas, base_scores, tile_values, tile_rows, tile_cols, send_rows, send_count, train_nodes, train_labels
):
    n = lax.axis_size("row")
    channels, local = base_scores.shape
    slots, size = send_rows.shape[1:]
    halo = slots * size
    high, low = dense(tile_rows, tile_cols, tile_values, local, halo)
    vmem = pl.BlockSpec(memory_space=pltpu.VMEM)
    smem = pl.BlockSpec(memory_space=pltpu.SMEM)
    hbm = pl.BlockSpec(memory_space=pl.ANY)
    whole = pltpu.VMEM((channels, local), F32)
    planes = (3, 1, 2, 1)
    boundary = [pltpu.VMEM((slots, size * p, channels), BF) for p in planes]
    return pl.pallas_call(
        functools.partial(spread_body, n),
        out_shape=jax.ShapeDtypeStruct((channels, local), F32),
        in_specs=[smem, smem, vmem, vmem, vmem, vmem, hbm, hbm],
        out_specs=vmem,
        scratch_shapes=[
            pltpu.VMEM(high.shape, BF),
            pltpu.VMEM(low.shape, BF),
            pltpu.VMEM((halo, local), BF),
            whole,
            whole,
            whole,
            *boundary,
            *boundary,
            pltpu.VMEM((8, 128), F32),
            pltpu.VMEM((n - 1, 8, 128), F32),
            pltpu.SemaphoreType.DMA((4, slots)),
            pltpu.SemaphoreType.DMA((4, slots)),
            pltpu.SemaphoreType.DMA((n - 1,)),
            pltpu.SemaphoreType.DMA((n - 1,)),
            pltpu.SemaphoreType.DMA((2,)),
        ],
        compiler_params=pltpu.CompilerParams(collective_id=0, has_side_effects=True, vmem_limit_bytes=40 << 20),
        name="spread",
    )(
        alphas, send_count, base_scores, send_rows,
        train_nodes.reshape(1, -1), train_labels.reshape(1, -1), high, low,
    )


def solution(mesh):
    return jax.shard_map(
        shards,
        mesh=mesh,
        in_specs=(
            P("sweep"), P(None, "row"), P("row", None, None), P("row"), P("row"),
            P("row", None, None), P("row", None), P("row"), P("row"),
        ),
        out_specs=P("sweep", "row"),
        check_vma=False,
    )
```

```python
import functools

import jax
import jax.numpy as jnp
from jax import lax
from jax.experimental import pallas as pl
from jax.experimental.pallas import tpu as pltpu
from jax.sharding import PartitionSpec as P

CHUNKS = 4
MESH = pl.DeviceIdType.MESH
BF = jnp.bfloat16
F32 = jnp.float32


def dot(a, b):
    return jnp.dot(a, b, preferred_element_type=F32)


def dot_nt(a, b, precision=None):
    return lax.dot_general(a, b, (((1,), (1,)), ((), ())), precision=precision, preferred_element_type=F32)


def dot_tn(a, b):
    return lax.dot_general(a, b, (((0,), (0,)), ((), ())), preferred_element_type=F32)


def split(x):
    high = x.astype(BF)
    return high, (x - high.astype(F32)).astype(BF)


def iota(shape, axis):
    return lax.broadcasted_iota(jnp.int32, shape, axis)


def ones_where(mask):
    return jnp.where(mask, 1.0, 0.0).astype(F32)


def bounded(index, size):
    return jnp.minimum(jnp.maximum(index, 0), size - 1)


def as_column(row):
    size = row.shape[1]
    eye = ones_where(iota((size, size), 0) == iota((size, size), 1))
    return dot_nt(eye, row, precision=lax.Precision.HIGHEST)


def tile_plan(rows, cols, row_blocks):
    count = rows.shape[1]
    key = (cols * row_blocks + rows).astype(F32)
    column = as_column(jnp.broadcast_to(key, (8, count)))[:, 0:1]
    square = (count, count)
    earlier = iota(square, 1) < iota(square, 0)
    twin = (key == column) & earlier
    rank = jnp.sum(ones_where((key < column) | twin), axis=1, keepdims=True)
    chained = jnp.sum(ones_where(twin), axis=1, keepdims=True) > 0.0
    placed = rank == iota(square, 1).astype(F32)
    order = jnp.sum(jnp.where(placed, iota(square, 0).astype(F32), 0.0), axis=0, keepdims=True)
    chain = jnp.sum(ones_where(placed & chained), axis=0, keepdims=True)
    block = iota(square, 1).astype(F32)
    upto = jnp.sum(ones_where(column <= block), axis=0, keepdims=True)
    any_tile = jnp.sum(ones_where(column == block), axis=0, keepdims=True) > 0.0
    last = jnp.where(any_tile, upto, 0.0)
    return order.astype(jnp.int32), chain.astype(jnp.int32), last.astype(jnp.int32)


def spread_body(
    n, alphas, counts, rows, cols, send_rows, nodes, labels, base_in, tiles, out,
    base, held, sums, high, low, pick, pick_high, pick_low, start, fixed, truth, plan, plan_s,
    sent0, sent1, sent2, sent3, sent4, got0, got1, got2, got3, got4,
    part, parts, send_sems, recv_sems, part_send, part_recv, load_sems,
):
    channels, local = base.shape
    count, tile, _ = held.shape
    row_blocks, col_blocks = local // tile, high.shape[0] // tile
    slots, size = send_rows.shape[1:]
    halo = slots * size
    reach = slots // 2
    offsets = [value for value in range(-reach, reach + 1) if value != 0]
    me = lax.axis_index("row")
    sent, got = (sent0, sent1, sent2, sent3, sent4), (got0, got1, got2, got3, got4)

    barrier = pltpu.get_barrier_semaphore()

    def greet(k, _):
        pl.semaphore_signal(barrier, inc=1, device_id={"row": lax.rem(me + k, n)}, device_id_type=MESH)
        return 0

    lax.fori_loop(1, n, greet, 0)
    base_load = pltpu.make_async_copy(base_in, base, load_sems.at[0])
    base_load.start()
    step = count // CHUNKS
    loads = []
    for chunk in range(CHUNKS):
        some = pl.ds(chunk * step, step)
        loads.append(pltpu.make_async_copy(tiles.at[some], held.at[some], load_sems.at[2 + chunk]))
        loads[-1].start()

    def inside(offset):
        return (me + offset >= 0) & (me + offset < n)

    for slot, offset in enumerate(offsets):

        @pl.when(jnp.logical_not(inside(offset)))
        def _():
            for buffer in got:
                buffer[slot] = jnp.zeros(buffer.shape[1:], buffer.dtype)

    def copy(turn, k):
        return pltpu.make_async_remote_copy(
            src_ref=sent[turn].at[k],
            dst_ref=got[turn].at[slots - 1 - k],
            send_sem=send_sems.at[turn, k],
            recv_sem=recv_sems.at[turn, slots - 1 - k],
            device_id={"row": me + offsets[k]},
            device_id_type=MESH,
        )

    def send(turn, picked):
        for k in range(slots):
            sent[turn][k] = picked[k * size : (k + 1) * size, :].astype(sent[turn].dtype)
        for k, offset in enumerate(offsets):

            @pl.when(inside(offset))
            def _():
                copy(turn, k).start()

    def receive(turn):
        for slot, offset in enumerate(offsets):

            @pl.when(inside(offset))
            def _():
                copy(turn, slots - 1 - slot).wait_recv()

        return jnp.concatenate([got[turn][slot] for slot in range(slots)], axis=0)

    def local_product(values):
        return dot(values, high[:local, :]) + dot(values, low[:local, :])

    def halo_product(values):
        return dot_tn(values, high[local:, :]) + dot_tn(values, low[local:, :])

    def picked_local(values):
        return dot_nt(pick_high[:, :local], values) + dot_nt(pick_low[:, :local], values)

    def picked_halo(values):
        return dot(pick_high[:, local:], values) + dot(pick_low[:, local:], values)

    wanted = as_column(send_rows[0].astype(F32)).astype(jnp.int32)
    column, place = iota((size, local), 1), iota((size, local), 0)
    for k in range(slots):
        live = (column == wanted[:, k : k + 1]) & (place < counts[0, k])
        pick[k * size : (k + 1) * size, :] = ones_where(live).astype(BF)
    labelled_count = nodes.shape[1]
    node = as_column(jnp.broadcast_to(nodes[...].astype(F32), (8, labelled_count)))[:, 0:1].astype(jnp.int32)
    placed = ones_where(iota((labelled_count, local), 1) == node).astype(BF)
    pick[halo:, :] = placed
    onehot = ones_where(iota((channels, labelled_count), 0) == labels[...]).astype(BF)
    truth[...] = dot(onehot, placed)
    labelled = dot(jnp.ones((8, labelled_count), BF), placed)
    free = 1.0 - labelled[0:1, :]
    base_load.wait()
    start[...] = labelled[0:1, :] * (truth[...] - base[...])
    values = start[...].astype(BF)
    first = dot_nt(pick[:halo, :], values)
    pl.semaphore_wait(barrier, n - 1)
    send(0, first)

    order, chain, last = tile_plan(rows[...], cols[...], row_blocks)
    plan[...] = jnp.zeros_like(plan)
    plan[0:1, :count] = order
    plan[1:2, :count] = chain
    plan[2:3, :count] = last
    plan_copy = pltpu.make_async_copy(plan, plan_s, load_sems.at[1])
    plan_copy.start()

    fixed[...] = truth[...] + free * base[...]
    rest = base[...]
    base_pick = jnp.zeros((pick.shape[0], channels), F32)
    for _ in range(3):
        term = rest.astype(BF)
        rest = rest - term.astype(F32)
        base_pick = base_pick + dot_nt(pick[...], term)
    truth_pick = dot_nt(pick[...], truth[...].astype(BF))
    labelled_pick = dot_nt(pick[...], labelled.astype(BF))[:, 0:1]
    live_pick = dot_nt(pick[...], jnp.ones((8, local), BF))[:, 0:1]
    free_pick = live_pick - labelled_pick
    start_pick = labelled_pick * (truth_pick - base_pick)
    fixed_pick = truth_pick + free_pick * base_pick

    sums[0] = jnp.zeros((tile, tile), F32)
    plan_copy.wait()
    for load in loads:
        load.wait()

    def add(k, running):
        keep = jnp.full((tile, tile), plan_s[1, k], jnp.int32) > 0
        running = jnp.where(keep, running, 0.0) + held[bounded(plan_s[0, k], count)].astype(F32)
        sums[k + 1] = running
        return running

    lax.fori_loop(0, count, add, jnp.zeros((tile, tile), F32))

    def settle(c, _):
        for r in range(row_blocks):
            high_part, low_part = split(sums[bounded(plan_s[2, c * row_blocks + r], count + 1)])
            where = (pl.ds(pl.multiple_of(c * tile, tile), tile), pl.ds(r * tile, tile))
            high[where] = high_part
            low[where] = low_part
        return 0

    lax.fori_loop(0, col_blocks, settle, 0)
    pick_high[...] = dot_nt(pick[...], high[...]).astype(BF)
    pick_low[...] = dot_nt(pick[...], low[...]).astype(BF)

    def folded(x):
        row = jnp.sum(x, axis=0, keepdims=True)
        return jnp.broadcast_to(jnp.sum(row, axis=1, keepdims=True), (1, 128))

    weight = alphas[0]
    picked = picked_local(values)
    total = local_product(values)
    edge = receive(0)
    picked = picked + picked_halo(edge)
    picked = (1.0 - weight) * start_pick + weight * picked
    send(1, picked)
    send(4, fixed_pick)
    total = total + halo_product(edge)
    values = ((1.0 - weight) * start[...] + weight * total).astype(BF)

    picked = picked_local(values)
    total = local_product(values)
    edge = receive(1)
    picked = picked + picked_halo(edge)
    picked = (1.0 - weight) * start_pick + weight * picked
    part[...] = jnp.zeros_like(part)
    part[0:1, :] = folded(jnp.abs(start_pick[halo:, :]))
    part[1:2, :] = folded(jnp.abs(picked[halo:, :]))

    def part_copy(k):
        return pltpu.make_async_remote_copy(
            src_ref=part,
            dst_ref=parts.at[k - 1],
            send_sem=part_send.at[k - 1],
            recv_sem=part_recv.at[k - 1],
            device_id={"row": lax.rem(me + k, n)},
            device_id_type=MESH,
        )

    def part_start(k, _):
        part_copy(k).start()
        return 0

    lax.fori_loop(1, n, part_start, 0)
    moving_pick = free_pick * picked
    send(2, moving_pick)
    total = total + halo_product(edge)
    moving = free * ((1.0 - weight) * start[...] + weight * total)

    def part_wait(k, _):
        part_copy(k).wait_recv()
        return 0

    lax.fori_loop(1, n, part_wait, 0)
    sums_all = part[...] + jnp.sum(parts[...], axis=0)
    entries = n * labelled_count * channels
    scale = (sums_all[0:1, 0:1] / entries) / (sums_all[1:2, 0:1] / entries + 1e-06)
    start[...] = fixed[...] + scale * moving
    anchored_pick = fixed_pick + scale * moving_pick

    weight = alphas[1]
    values = start[...].astype(BF)
    picked = picked_local(values)
    fixed_edge = receive(4)
    edge = (fixed_edge + scale * receive(2)).astype(BF)
    picked = picked + picked_halo(edge)
    send(3, truth_pick + free_pick * ((1.0 - weight) * anchored_pick + weight * picked))
    total = local_product(values) + halo_product(edge)
    values = (truth[...] + free * ((1.0 - weight) * start[...] + weight * total)).astype(BF)

    total = local_product(values)
    total = total + halo_product(receive(3))
    out[...] = truth[...] + free * ((1.0 - weight) * start[...] + weight * total)

    for turn in range(len(sent)):
        for k, offset in enumerate(offsets):

            @pl.when(inside(offset))
            def _():
                copy(turn, k).wait_send()

    def part_end(k, _):
        part_copy(k).wait_send()
        return 0

    lax.fori_loop(1, n, part_end, 0)


def shards(
    alphas, base_scores, tile_values, tile_rows, tile_cols, send_rows, send_count, train_nodes, train_labels
):
    n = lax.axis_size("row")
    channels, local = base_scores.shape
    slots, size = send_rows.shape[1:]
    count, tile, _ = tile_values.shape
    halo = slots * size
    picks = halo + train_nodes.shape[0]
    vmem = pl.BlockSpec(memory_space=pltpu.VMEM)
    smem = pl.BlockSpec(memory_space=pltpu.SMEM)
    hbm = pl.BlockSpec(memory_space=pl.ANY)
    whole = pltpu.VMEM((channels, local), F32)
    lanes = -(-count // 128) * 128
    boundary = [pltpu.VMEM((slots, size, channels), kind) for kind in (BF, BF, F32, BF, F32)]
    return pl.pallas_call(
        functools.partial(spread_body, n),
        out_shape=jax.ShapeDtypeStruct((channels, local), F32),
        in_specs=[smem, smem, vmem, vmem, vmem, vmem, vmem, hbm, hbm],
        out_specs=vmem,
        scratch_shapes=[
            whole,
            pltpu.VMEM(tile_values.shape, BF),
            pltpu.VMEM((count + 1, tile, tile), F32),
            pltpu.VMEM((local + halo, local), BF),
            pltpu.VMEM((local + halo, local), BF),
            pltpu.VMEM((picks, local), BF),
            pltpu.VMEM((picks, local + halo), BF),
            pltpu.VMEM((picks, local + halo), BF),
            whole,
            whole,
            whole,
            pltpu.VMEM((8, lanes), jnp.int32),
            pltpu.SMEM((8, lanes), jnp.int32),
            *boundary,
            *boundary,
            pltpu.VMEM((8, 128), F32),
            pltpu.VMEM((n - 1, 8, 128), F32),
            pltpu.SemaphoreType.DMA((5, slots)),
            pltpu.SemaphoreType.DMA((5, slots)),
            pltpu.SemaphoreType.DMA((n - 1,)),
            pltpu.SemaphoreType.DMA((n - 1,)),
            pltpu.SemaphoreType.DMA((2 + CHUNKS,)),
        ],
        compiler_params=pltpu.CompilerParams(collective_id=0, has_side_effects=True, vmem_limit_bytes=60 << 20),
        name="spread",
    )(
        alphas, send_count, tile_rows.reshape(1, -1), tile_cols.reshape(1, -1), send_rows,
        train_nodes.reshape(1, -1), train_labels.reshape(1, -1), base_scores, tile_values,
    )


def solution(mesh):
    return jax.shard_map(
        shards,
        mesh=mesh,
        in_specs=(
            P("sweep"), P(None, "row"), P("row", None, None), P("row"), P("row"),
            P("row", None, None), P("row", None), P("row"), P("row"),
        ),
        out_specs=P("sweep", "row"),
        check_vma=False,
    )
```

```python
import functools

import jax
import jax.numpy as jnp
from jax import lax
from jax.experimental import pallas as pl
from jax.experimental.pallas import tpu as pltpu
from jax.sharding import PartitionSpec as P

CHUNKS = 4
WIDTH = 256
LIMIT = 56 << 20
MESH = pl.DeviceIdType.MESH
BF = jnp.bfloat16
F32 = jnp.float32


def dot(a, b):
    return jnp.dot(a, b, preferred_element_type=F32)


def dot_nt(a, b, precision=None):
    return lax.dot_general(a, b, (((1,), (1,)), ((), ())), precision=precision, preferred_element_type=F32)


def dot_tn(a, b):
    return lax.dot_general(a, b, (((0,), (0,)), ((), ())), preferred_element_type=F32)


def split(x):
    high = x.astype(BF)
    return high, (x - high.astype(F32)).astype(BF)


def iota(shape, axis):
    return lax.broadcasted_iota(jnp.int32, shape, axis)


def ones_where(mask):
    return jnp.where(mask, 1.0, 0.0).astype(F32)


def bounded(index, size):
    return jnp.minimum(jnp.maximum(index, 0), size - 1)


def as_column(row):
    size = row.shape[1]
    eye = ones_where(iota((size, size), 0) == iota((size, size), 1))
    return dot_nt(eye, row, precision=lax.Precision.HIGHEST)


def tile_plan(rows, cols, row_blocks):
    count = rows.shape[1]
    key = (cols * row_blocks + rows).astype(F32)
    column = as_column(jnp.broadcast_to(key, (8, count)))[:, 0:1]
    square = (count, count)
    earlier = iota(square, 1) < iota(square, 0)
    twin = (key == column) & earlier
    rank = jnp.sum(ones_where((key < column) | twin), axis=1, keepdims=True)
    chained = jnp.sum(ones_where(twin), axis=1, keepdims=True) > 0.0
    placed = rank == iota(square, 1).astype(F32)
    order = jnp.sum(jnp.where(placed, iota(square, 0).astype(F32), 0.0), axis=0, keepdims=True)
    chain = jnp.sum(ones_where(placed & chained), axis=0, keepdims=True)
    block = iota(square, 1).astype(F32)
    upto = jnp.sum(ones_where(column <= block), axis=0, keepdims=True)
    any_tile = jnp.sum(ones_where(column == block), axis=0, keepdims=True) > 0.0
    last = jnp.where(any_tile, upto, 0.0)
    return order.astype(jnp.int32), chain.astype(jnp.int32), last.astype(jnp.int32)


def spread_body(
    n, alphas, counts, rows, cols, send_rows, nodes, labels, base_in, tiles, out,
    base, held, sums, high, low, pick, pick_high, pick_low, start, fixed, truth, free, wide0, wide1, total, plan, plan_s,
    sent0, sent1, sent2, sent3, sent4, got0, got1, got2, got3, got4,
    part, parts, send_sems, recv_sems, part_send, part_recv, load_sems,
):
    channels, local = base.shape
    count, tile, _ = held.shape
    row_blocks, col_blocks = local // tile, high.shape[0] // tile
    slots, size = send_rows.shape[1:]
    halo = slots * size
    reach = slots // 2
    offsets = [value for value in range(-reach, reach + 1) if value != 0]
    me = lax.axis_index("row")
    sent, got = (sent0, sent1, sent2, sent3, sent4), (got0, got1, got2, got3, got4)

    barrier = pltpu.get_barrier_semaphore()

    def greet(k, _):
        pl.semaphore_signal(barrier, inc=1, device_id={"row": lax.rem(me + k, n)}, device_id_type=MESH)
        return 0

    lax.fori_loop(1, n, greet, 0)
    base_load = pltpu.make_async_copy(base_in, base, load_sems.at[0])
    base_load.start()
    step = count // CHUNKS
    loads = []
    for chunk in range(CHUNKS):
        some = pl.ds(chunk * step, step)
        loads.append(pltpu.make_async_copy(tiles.at[some], held.at[some], load_sems.at[2 + chunk]))
        loads[-1].start()

    def inside(offset):
        return (me + offset >= 0) & (me + offset < n)

    for slot, offset in enumerate(offsets):

        @pl.when(jnp.logical_not(inside(offset)))
        def _():
            for buffer in got:
                buffer[slot] = jnp.zeros(buffer.shape[1:], buffer.dtype)

    def copy(turn, k):
        return pltpu.make_async_remote_copy(
            src_ref=sent[turn].at[k],
            dst_ref=got[turn].at[slots - 1 - k],
            send_sem=send_sems.at[turn, k],
            recv_sem=recv_sems.at[turn, slots - 1 - k],
            device_id={"row": me + offsets[k]},
            device_id_type=MESH,
        )

    def send(turn, picked):
        for k in range(slots):
            sent[turn][k] = picked[k * size : (k + 1) * size, :].astype(sent[turn].dtype)
        for k, offset in enumerate(offsets):

            @pl.when(inside(offset))
            def _():
                copy(turn, k).start()

    def receive(turn):
        for slot, offset in enumerate(offsets):

            @pl.when(inside(offset))
            def _():
                copy(turn, slots - 1 - slot).wait_recv()

        return jnp.concatenate([got[turn][slot] for slot in range(slots)], axis=0)

    def over_columns(step):
        def one(j, _):
            step(pl.ds(pl.multiple_of(j * WIDTH, WIDTH), WIDTH))
            return 0

        lax.fori_loop(0, local // WIDTH, one, 0)

    def product(values, rows, columns):
        return dot(values, high[rows, columns]) + dot(values, low[rows, columns])

    def picked_local(values):
        return dot_nt(pick_high[:, :local], values) + dot_nt(pick_low[:, :local], values)

    def picked_halo(values):
        return dot(pick_high[:, local:], values) + dot(pick_low[:, local:], values)

    order, chain, last = tile_plan(rows[...], cols[...], row_blocks)
    plan[...] = jnp.zeros_like(plan)
    plan[0:1, :count] = order
    plan[1:2, :count] = chain
    plan[2:3, :count] = last
    plan_copy = pltpu.make_async_copy(plan, plan_s, load_sems.at[1])
    plan_copy.start()

    wanted = as_column(send_rows[0].astype(F32)).astype(jnp.int32)
    column, place = iota((size, local), 1), iota((size, local), 0)
    for k in range(slots):
        live = (column == wanted[:, k : k + 1]) & (place < counts[0, k])
        pick[k * size : (k + 1) * size, :] = ones_where(live).astype(BF)
    labelled_count = nodes.shape[1]
    node = as_column(jnp.broadcast_to(nodes[...].astype(F32), (8, labelled_count)))[:, 0:1].astype(jnp.int32)
    placed = ones_where(iota((labelled_count, local), 1) == node).astype(BF)
    pick[halo:, :] = placed
    onehot = ones_where(iota((channels, labelled_count), 0) == labels[...]).astype(BF)
    truth[...] = dot(onehot, placed)
    labelled = dot(jnp.ones((8, labelled_count), BF), placed)
    free[...] = 1.0 - labelled
    base_load.wait()
    start[...] = labelled[0:1, :] * (truth[...] - base[...])
    wide0[:, :local] = start[...].astype(BF)
    first = dot_nt(pick[:halo, :], wide0[:, :local])
    pl.semaphore_wait(barrier, n - 1)
    send(0, first)

    fixed[...] = truth[...] + free[0:1, :] * base[...]
    rest = base[...]
    base_pick = jnp.zeros((pick.shape[0], channels), F32)
    for _ in range(3):
        term = rest.astype(BF)
        rest = rest - term.astype(F32)
        base_pick = base_pick + dot_nt(pick[...], term)
    truth_pick = dot_nt(pick[...], truth[...].astype(BF))
    labelled_pick = dot_nt(pick[...], labelled.astype(BF))[:, 0:1]
    live_pick = dot_nt(pick[...], jnp.ones((8, local), BF))[:, 0:1]
    free_pick = live_pick - labelled_pick
    start_pick = labelled_pick * (truth_pick - base_pick)
    fixed_pick = truth_pick + free_pick * base_pick

    sums[0] = jnp.zeros((tile, tile), F32)
    plan_copy.wait()
    for load in loads:
        load.wait()

    def add(k, running):
        keep = jnp.full((tile, tile), plan_s[1, k], jnp.int32) > 0
        running = jnp.where(keep, running, 0.0) + held[bounded(plan_s[0, k], count)].astype(F32)
        sums[k + 1] = running
        return running

    lax.fori_loop(0, count, add, jnp.zeros((tile, tile), F32), unroll=8)

    def settle(c, _):
        for r in range(row_blocks):
            high_part, low_part = split(sums[bounded(plan_s[2, c * row_blocks + r], count + 1)])
            where = (pl.ds(pl.multiple_of(c * tile, tile), tile), pl.ds(r * tile, tile))
            high[where] = high_part
            low[where] = low_part
        return 0

    lax.fori_loop(0, col_blocks, settle, 0)
    group = (local + halo) // 3

    def pick_columns(j, _):
        columns = pl.ds(pl.multiple_of(j * group, tile), group)
        pick_high[:, columns] = dot_nt(pick[...], high[columns, :]).astype(BF)
        pick_low[:, columns] = dot_nt(pick[...], low[columns, :]).astype(BF)
        return 0

    lax.fori_loop(0, 3, pick_columns, 0)

    def folded(x):
        row = jnp.sum(x, axis=0, keepdims=True)
        return jnp.broadcast_to(jnp.sum(row, axis=1, keepdims=True), (1, 128))

    weight = alphas[0]
    picked = picked_local(wide0[:, :local])
    edge = receive(0)
    picked = picked + picked_halo(edge)
    picked = (1.0 - weight) * start_pick + weight * picked
    send(1, picked)
    send(4, fixed_pick)
    wide0[:, local:] = edge.T

    def first_hop(columns):
        spread = product(wide0[...], slice(None), columns)
        wide1[:, columns] = ((1.0 - weight) * start[:, columns] + weight * spread).astype(BF)

    over_columns(first_hop)

    picked = picked_local(wide1[:, :local])
    edge = receive(1)
    picked = picked + picked_halo(edge)
    picked = (1.0 - weight) * start_pick + weight * picked
    part[...] = jnp.zeros_like(part)
    part[0:1, :] = folded(jnp.abs(start_pick[halo:, :]))
    part[1:2, :] = folded(jnp.abs(picked[halo:, :]))

    def part_copy(k):
        return pltpu.make_async_remote_copy(
            src_ref=part,
            dst_ref=parts.at[k - 1],
            send_sem=part_send.at[k - 1],
            recv_sem=part_recv.at[k - 1],
            device_id={"row": lax.rem(me + k, n)},
            device_id_type=MESH,
        )

    def part_start(k, _):
        part_copy(k).start()
        return 0

    lax.fori_loop(1, n, part_start, 0)
    moving_pick = free_pick * picked
    send(2, moving_pick)
    wide1[:, local:] = edge.T

    def second_hop(columns):
        spread = product(wide1[...], slice(None), columns)
        total[:, columns] = free[0:1, columns] * ((1.0 - weight) * start[:, columns] + weight * spread)

    over_columns(second_hop)

    def part_wait(k, _):
        part_copy(k).wait_recv()
        return 0

    lax.fori_loop(1, n, part_wait, 0)
    sums_all = part[...] + jnp.sum(parts[...], axis=0)
    entries = n * labelled_count * channels
    scale = (sums_all[0:1, 0:1] / entries) / (sums_all[1:2, 0:1] / entries + 1e-06)
    start[...] = fixed[...] + scale * total[...]
    wide0[:, :local] = start[...].astype(BF)
    anchored_pick = fixed_pick + scale * moving_pick

    weight = alphas[1]
    picked = picked_local(wide0[:, :local])
    fixed_edge = receive(4)
    edge = (fixed_edge + scale * receive(2)).astype(BF)
    picked = picked + picked_halo(edge)
    send(3, truth_pick + free_pick * ((1.0 - weight) * anchored_pick + weight * picked))
    wide0[:, local:] = edge.T

    def third_hop(columns):
        spread = product(wide0[...], slice(None), columns)
        smoothed = (1.0 - weight) * start[:, columns] + weight * spread
        wide1[:, columns] = (truth[:, columns] + free[0:1, columns] * smoothed).astype(BF)

    over_columns(third_hop)

    def fourth_hop(columns):
        total[:, columns] = product(wide1[:, :local], slice(0, local), columns)

    over_columns(fourth_hop)
    wide1[:, local:] = receive(3).T

    def finish(columns):
        spread = total[:, columns] + product(wide1[:, local:], slice(local, None), columns)
        smoothed = (1.0 - weight) * start[:, columns] + weight * spread
        out[:, columns] = truth[:, columns] + free[0:1, columns] * smoothed

    over_columns(finish)

    for turn in range(len(sent)):
        for k, offset in enumerate(offsets):

            @pl.when(inside(offset))
            def _():
                copy(turn, k).wait_send()

    def part_end(k, _):
        part_copy(k).wait_send()
        return 0

    lax.fori_loop(1, n, part_end, 0)


def shards(
    alphas, base_scores, tile_values, tile_rows, tile_cols, send_rows, send_count, train_nodes, train_labels
):
    n = lax.axis_size("row")
    channels, local = base_scores.shape
    slots, size = send_rows.shape[1:]
    count, tile, _ = tile_values.shape
    halo = slots * size
    picks = halo + train_nodes.shape[0]
    vmem = pl.BlockSpec(memory_space=pltpu.VMEM)
    smem = pl.BlockSpec(memory_space=pltpu.SMEM)
    hbm = pl.BlockSpec(memory_space=pl.ANY)
    whole = pltpu.VMEM((channels, local), F32)
    wide = pltpu.VMEM((channels, local + halo), BF)
    lanes = -(-count // 128) * 128
    boundary = [pltpu.VMEM((slots, size, channels), kind) for kind in (BF, BF, F32, BF, F32)]
    return pl.pallas_call(
        functools.partial(spread_body, n),
        out_shape=pltpu.VMEM((channels, local), F32),
        in_specs=[smem, smem, vmem, vmem, vmem, vmem, vmem, hbm, hbm],
        out_specs=vmem,
        scratch_shapes=[
            whole,
            pltpu.VMEM(tile_values.shape, BF),
            pltpu.VMEM((count + 1, tile, tile), F32),
            pltpu.VMEM((local + halo, local), BF),
            pltpu.VMEM((local + halo, local), BF),
            pltpu.VMEM((picks, local), BF),
            pltpu.VMEM((picks, local + halo), BF),
            pltpu.VMEM((picks, local + halo), BF),
            whole,
            whole,
            whole,
            pltpu.VMEM((8, local), F32),
            wide,
            wide,
            whole,
            pltpu.VMEM((8, lanes), jnp.int32),
            pltpu.SMEM((8, lanes), jnp.int32),
            *boundary,
            *boundary,
            pltpu.VMEM((8, 128), F32),
            pltpu.VMEM((n - 1, 8, 128), F32),
            pltpu.SemaphoreType.DMA((5, slots)),
            pltpu.SemaphoreType.DMA((5, slots)),
            pltpu.SemaphoreType.DMA((n - 1,)),
            pltpu.SemaphoreType.DMA((n - 1,)),
            pltpu.SemaphoreType.DMA((2 + CHUNKS,)),
        ],
        compiler_params=pltpu.CompilerParams(collective_id=0, has_side_effects=True, vmem_limit_bytes=LIMIT),
        name="spread",
    )(
        alphas, send_count, tile_rows.reshape(1, -1), tile_cols.reshape(1, -1), send_rows,
        train_nodes.reshape(1, -1), train_labels.reshape(1, -1), base_scores, tile_values,
    )


def solution(mesh):
    return jax.shard_map(
        shards,
        mesh=mesh,
        in_specs=(
            P("sweep"), P(None, "row"), P("row", None, None), P("row"), P("row"),
            P("row", None, None), P("row", None), P("row"), P("row"),
        ),
        out_specs=P("sweep", "row"),
        check_vma=False,
    )
```

```python
import functools

import jax
import jax.numpy as jnp
from jax import lax
from jax.experimental import pallas as pl
from jax.experimental.pallas import tpu as pltpu
from jax.sharding import PartitionSpec as P

CHUNKS = 4
WIDTH = 256
LIMIT = 56 << 20
MESH = pl.DeviceIdType.MESH
BF = jnp.bfloat16
F32 = jnp.float32


def dot(a, b):
    return jnp.dot(a, b, preferred_element_type=F32)


def dot_nt(a, b, precision=None):
    return lax.dot_general(a, b, (((1,), (1,)), ((), ())), precision=precision, preferred_element_type=F32)


def dot_tn(a, b):
    return lax.dot_general(a, b, (((0,), (0,)), ((), ())), preferred_element_type=F32)


def split(x):
    high = x.astype(BF)
    return high, (x - high.astype(F32)).astype(BF)


def iota(shape, axis):
    return lax.broadcasted_iota(jnp.int32, shape, axis)


def ones_where(mask):
    return jnp.where(mask, 1.0, 0.0).astype(F32)


def bounded(index, size):
    return jnp.minimum(jnp.maximum(index, 0), size - 1)


def as_column(row):
    size = row.shape[1]
    eye = ones_where(iota((size, size), 0) == iota((size, size), 1))
    return dot_nt(eye, row, precision=lax.Precision.HIGHEST)


def tile_plan(rows, cols, row_blocks):
    count = rows.shape[1]
    key = (cols * row_blocks + rows).astype(F32)
    column = as_column(jnp.broadcast_to(key, (8, count)))[:, 0:1]
    square = (count, count)
    earlier = iota(square, 1) < iota(square, 0)
    twin = (key == column) & earlier
    rank = jnp.sum(ones_where((key < column) | twin), axis=1, keepdims=True)
    chained = jnp.sum(ones_where(twin), axis=1, keepdims=True) > 0.0
    placed = rank == iota(square, 1).astype(F32)
    order = jnp.sum(jnp.where(placed, iota(square, 0).astype(F32), 0.0), axis=0, keepdims=True)
    chain = jnp.sum(ones_where(placed & chained), axis=0, keepdims=True)
    block = iota(square, 1).astype(F32)
    upto = jnp.sum(ones_where(column <= block), axis=0, keepdims=True)
    any_tile = jnp.sum(ones_where(column == block), axis=0, keepdims=True) > 0.0
    last = jnp.where(any_tile, upto, 0.0)
    return order.astype(jnp.int32), chain.astype(jnp.int32), last.astype(jnp.int32)


def spread_body(
    n, alphas, counts, rows, cols, send_rows, nodes, labels, base_in, tiles, out,
    base, held, sums, high, low, pick, pick_high, pick_low, start, fixed, truth, free, wide0, wide1, total, plan, plan_s,
    sent0, sent1, sent2, sent3, sent4, got0, got1, got2, got3, got4,
    part, parts, send_sems, recv_sems, part_send, part_recv, load_sems,
):
    channels, local = base.shape
    count, tile, _ = held.shape
    row_blocks, col_blocks = local // tile, high.shape[0] // tile
    slots, size = send_rows.shape[1:]
    halo = slots * size
    reach = slots // 2
    offsets = [value for value in range(-reach, reach + 1) if value != 0]
    me = lax.axis_index("row")
    sent, got = (sent0, sent1, sent2, sent3, sent4), (got0, got1, got2, got3, got4)

    barrier = pltpu.get_barrier_semaphore()

    def greet(k, _):
        pl.semaphore_signal(barrier, inc=1, device_id={"row": lax.rem(me + k, n)}, device_id_type=MESH)
        return 0

    lax.fori_loop(1, n, greet, 0)
    base_load = pltpu.make_async_copy(base_in, base, load_sems.at[0])
    base_load.start()
    step = count // CHUNKS
    loads = []
    for chunk in range(CHUNKS):
        some = pl.ds(chunk * step, step)
        loads.append(pltpu.make_async_copy(tiles.at[some], held.at[some], load_sems.at[2 + chunk]))
        loads[-1].start()

    def inside(offset):
        return (me + offset >= 0) & (me + offset < n)

    for slot, offset in enumerate(offsets):

        @pl.when(jnp.logical_not(inside(offset)))
        def _():
            for buffer in got:
                buffer[slot] = jnp.zeros(buffer.shape[1:], buffer.dtype)

    def copy(turn, k):
        return pltpu.make_async_remote_copy(
            src_ref=sent[turn].at[k],
            dst_ref=got[turn].at[slots - 1 - k],
            send_sem=send_sems.at[turn, k],
            recv_sem=recv_sems.at[turn, slots - 1 - k],
            device_id={"row": me + offsets[k]},
            device_id_type=MESH,
        )

    def send(turn, picked):
        for k in range(slots):
            sent[turn][k] = picked[k * size : (k + 1) * size, :].astype(sent[turn].dtype)
        for k, offset in enumerate(offsets):

            @pl.when(inside(offset))
            def _():
                copy(turn, k).start()

    def receive(turn):
        for slot, offset in enumerate(offsets):

            @pl.when(inside(offset))
            def _():
                copy(turn, slots - 1 - slot).wait_recv()

        return jnp.concatenate([got[turn][slot] for slot in range(slots)], axis=0)

    def over_columns(step):
        def one(j, _):
            step(pl.ds(pl.multiple_of(j * WIDTH, WIDTH), WIDTH))
            return 0

        lax.fori_loop(0, local // WIDTH, one, 0)

    def product(values, rows, columns):
        return dot(values, high[rows, columns]) + dot(values, low[rows, columns])

    def picked_local(values):
        return dot_nt(pick_high[:, :local], values) + dot_nt(pick_low[:, :local], values)

    def picked_halo(values):
        return dot(pick_high[:, local:], values) + dot(pick_low[:, local:], values)

    order, chain, last = tile_plan(rows[...], cols[...], row_blocks)
    plan[...] = jnp.zeros_like(plan)
    plan[0:1, :count] = order
    plan[1:2, :count] = chain
    plan[2:3, :count] = last
    plan_copy = pltpu.make_async_copy(plan, plan_s, load_sems.at[1])
    plan_copy.start()

    wanted = as_column(send_rows[0].astype(F32)).astype(jnp.int32)
    column, place = iota((size, local), 1), iota((size, local), 0)
    for k in range(slots):
        live = (column == wanted[:, k : k + 1]) & (place < counts[0, k])
        pick[k * size : (k + 1) * size, :] = ones_where(live).astype(BF)
    labelled_count = nodes.shape[1]
    node = as_column(jnp.broadcast_to(nodes[...].astype(F32), (8, labelled_count)))[:, 0:1].astype(jnp.int32)
    placed = ones_where(iota((labelled_count, local), 1) == node).astype(BF)
    pick[halo:, :] = placed
    onehot = ones_where(iota((channels, labelled_count), 0) == labels[...]).astype(BF)
    truth[...] = dot(onehot, placed)
    labelled = dot(jnp.ones((8, labelled_count), BF), placed)
    free[...] = 1.0 - labelled
    base_load.wait()
    start[...] = labelled[0:1, :] * (truth[...] - base[...])
    wide0[:, :local] = start[...].astype(BF)
    first = dot_nt(pick[:halo, :], wide0[:, :local])
    pl.semaphore_wait(barrier, n - 1)
    send(0, first)

    fixed[...] = truth[...] + free[0:1, :] * base[...]
    rest = base[...]
    base_pick = jnp.zeros((pick.shape[0], channels), F32)
    for _ in range(3):
        term = rest.astype(BF)
        rest = rest - term.astype(F32)
        base_pick = base_pick + dot_nt(pick[...], term)
    truth_pick = dot_nt(pick[...], truth[...].astype(BF))
    labelled_pick = dot_nt(pick[...], labelled.astype(BF))[:, 0:1]
    live_pick = dot_nt(pick[...], jnp.ones((8, local), BF))[:, 0:1]
    free_pick = live_pick - labelled_pick
    start_pick = labelled_pick * (truth_pick - base_pick)
    fixed_pick = truth_pick + free_pick * base_pick

    sums[0] = jnp.zeros((tile, tile), F32)
    plan_copy.wait()
    for load in loads:
        load.wait()

    def add(k, running):
        keep = jnp.full((tile, tile), plan_s[1, k], jnp.int32) > 0
        running = jnp.where(keep, running, 0.0) + held[bounded(plan_s[0, k], count)].astype(F32)
        sums[k + 1] = running
        return running

    lax.fori_loop(0, count, add, jnp.zeros((tile, tile), F32), unroll=8)

    def settle(c, _):
        for r in range(row_blocks):
            high_part, low_part = split(sums[bounded(plan_s[2, c * row_blocks + r], count + 1)])
            where = (pl.ds(pl.multiple_of(c * tile, tile), tile), pl.ds(r * tile, tile))
            high[where] = high_part
            low[where] = low_part
        return 0

    lax.fori_loop(0, col_blocks, settle, 0)
    group = (local + halo) // 3

    def pick_columns(j, _):
        columns = pl.ds(pl.multiple_of(j * group, tile), group)
        pick_high[:, columns] = dot_nt(pick[...], high[columns, :]).astype(BF)
        pick_low[:, columns] = dot_nt(pick[...], low[columns, :]).astype(BF)
        return 0

    lax.fori_loop(0, 3, pick_columns, 0)

    def folded(x):
        row = jnp.sum(x, axis=0, keepdims=True)
        return jnp.sum(row, axis=1, keepdims=True)

    weight = alphas[0]
    picked = picked_local(wide0[:, :local])
    edge = receive(0)
    picked = picked + picked_halo(edge)
    picked = (1.0 - weight) * start_pick + weight * picked
    send(1, picked)
    send(4, fixed_pick)
    wide0[:, local:] = edge.T

    def first_hop(columns):
        spread = product(wide0[...], slice(None), columns)
        wide1[:, columns] = ((1.0 - weight) * start[:, columns] + weight * spread).astype(BF)

    over_columns(first_hop)

    picked = picked_local(wide1[:, :local])
    edge = receive(1)
    picked = picked + picked_halo(edge)
    picked = (1.0 - weight) * start_pick + weight * picked
    mass, spread_mass = folded(jnp.abs(start_pick[halo:, :])), folded(jnp.abs(picked[halo:, :]))
    part[...] = jnp.where(iota((1, 128), 1) < 64, mass, spread_mass)

    def part_copy(k):
        return pltpu.make_async_remote_copy(
            src_ref=part,
            dst_ref=parts.at[k - 1],
            send_sem=part_send.at[k - 1],
            recv_sem=part_recv.at[k - 1],
            device_id={"row": lax.rem(me + k, n)},
            device_id_type=MESH,
        )

    def part_start(k, _):
        part_copy(k).start()
        return 0

    lax.fori_loop(1, n, part_start, 0)
    moving_pick = free_pick * picked
    send(2, moving_pick)
    wide1[:, local:] = edge.T

    def second_hop(columns):
        spread = product(wide1[...], slice(None), columns)
        total[:, columns] = free[0:1, columns] * ((1.0 - weight) * start[:, columns] + weight * spread)

    over_columns(second_hop)

    def part_wait(k, _):
        part_copy(k).wait_recv()
        return 0

    lax.fori_loop(1, n, part_wait, 0)
    sums_all = part[...] + jnp.sum(parts[...], axis=0)
    entries = n * labelled_count * channels
    scale = (sums_all[:, 0:1] / entries) / (sums_all[:, 64:65] / entries + 1e-06)
    start[...] = fixed[...] + scale * total[...]
    wide0[:, :local] = start[...].astype(BF)
    anchored_pick = fixed_pick + scale * moving_pick

    weight = alphas[1]
    picked = picked_local(wide0[:, :local])
    fixed_edge = receive(4)
    edge = (fixed_edge + scale * receive(2)).astype(BF)
    picked = picked + picked_halo(edge)
    send(3, truth_pick + free_pick * ((1.0 - weight) * anchored_pick + weight * picked))
    wide0[:, local:] = edge.T

    def third_hop(columns):
        spread = product(wide0[...], slice(None), columns)
        smoothed = (1.0 - weight) * start[:, columns] + weight * spread
        wide1[:, columns] = (truth[:, columns] + free[0:1, columns] * smoothed).astype(BF)

    over_columns(third_hop)

    def fourth_hop(columns):
        total[:, columns] = product(wide1[:, :local], slice(0, local), columns)

    over_columns(fourth_hop)
    wide1[:, local:] = receive(3).T

    def finish(columns):
        spread = total[:, columns] + product(wide1[:, local:], slice(local, None), columns)
        smoothed = (1.0 - weight) * start[:, columns] + weight * spread
        out[:, columns] = truth[:, columns] + free[0:1, columns] * smoothed

    over_columns(finish)

    for turn in range(len(sent)):
        for k, offset in enumerate(offsets):

            @pl.when(inside(offset))
            def _():
                copy(turn, k).wait_send()

    def part_end(k, _):
        part_copy(k).wait_send()
        return 0

    lax.fori_loop(1, n, part_end, 0)


def shards(
    alphas, base_scores, tile_values, tile_rows, tile_cols, send_rows, send_count, train_nodes, train_labels
):
    n = lax.axis_size("row")
    channels, local = base_scores.shape
    slots, size = send_rows.shape[1:]
    count, tile, _ = tile_values.shape
    halo = slots * size
    picks = halo + train_nodes.shape[0]
    vmem = pl.BlockSpec(memory_space=pltpu.VMEM)
    smem = pl.BlockSpec(memory_space=pltpu.SMEM)
    hbm = pl.BlockSpec(memory_space=pl.ANY)
    whole = pltpu.VMEM((channels, local), F32)
    wide = pltpu.VMEM((channels, local + halo), BF)
    lanes = -(-count // 128) * 128
    boundary = [pltpu.VMEM((slots, size, channels), kind) for kind in (BF, BF, F32, BF, F32)]
    return pl.pallas_call(
        functools.partial(spread_body, n),
        out_shape=pltpu.VMEM((channels, local), F32),
        in_specs=[smem, smem, vmem, vmem, vmem, vmem, vmem, hbm, hbm],
        out_specs=vmem,
        scratch_shapes=[
            whole,
            pltpu.VMEM(tile_values.shape, BF),
            pltpu.VMEM((count + 1, tile, tile), F32),
            pltpu.VMEM((local + halo, local), BF),
            pltpu.VMEM((local + halo, local), BF),
            pltpu.VMEM((picks, local), BF),
            pltpu.VMEM((picks, local + halo), BF),
            pltpu.VMEM((picks, local + halo), BF),
            whole,
            whole,
            whole,
            pltpu.VMEM((8, local), F32),
            wide,
            wide,
            whole,
            pltpu.VMEM((8, lanes), jnp.int32),
            pltpu.SMEM((8, lanes), jnp.int32),
            *boundary,
            *boundary,
            pltpu.VMEM((1, 128), F32),
            pltpu.VMEM((n - 1, 1, 128), F32),
            pltpu.SemaphoreType.DMA((5, slots)),
            pltpu.SemaphoreType.DMA((5, slots)),
            pltpu.SemaphoreType.DMA((n - 1,)),
            pltpu.SemaphoreType.DMA((n - 1,)),
            pltpu.SemaphoreType.DMA((2 + CHUNKS,)),
        ],
        compiler_params=pltpu.CompilerParams(collective_id=0, has_side_effects=True, vmem_limit_bytes=LIMIT),
        name="spread",
    )(
        alphas, send_count, tile_rows.reshape(1, -1), tile_cols.reshape(1, -1), send_rows,
        train_nodes.reshape(1, -1), train_labels.reshape(1, -1), base_scores, tile_values,
    )


def solution(mesh):
    return jax.shard_map(
        shards,
        mesh=mesh,
        in_specs=(
            P("sweep"), P(None, "row"), P("row", None, None), P("row"), P("row"),
            P("row", None, None), P("row", None), P("row"), P("row"),
        ),
        out_specs=P("sweep", "row"),
        check_vma=False,
    )
```

```python
import functools

import jax
import jax.numpy as jnp
from jax import lax
from jax.experimental import pallas as pl
from jax.experimental.pallas import tpu as pltpu
from jax.sharding import PartitionSpec as P

CHUNKS = 4
WIDTH = 1024
LIMIT = 56 << 20
MESH = pl.DeviceIdType.MESH
BF = jnp.bfloat16
F32 = jnp.float32


def dot(a, b):
    return jnp.dot(a, b, preferred_element_type=F32)


def dot_nt(a, b, precision=None):
    return lax.dot_general(a, b, (((1,), (1,)), ((), ())), precision=precision, preferred_element_type=F32)


def dot_tn(a, b):
    return lax.dot_general(a, b, (((0,), (0,)), ((), ())), preferred_element_type=F32)


def split(x):
    high = x.astype(BF)
    return high, (x - high.astype(F32)).astype(BF)


def iota(shape, axis):
    return lax.broadcasted_iota(jnp.int32, shape, axis)


def ones_where(mask):
    return jnp.where(mask, 1.0, 0.0).astype(F32)


def bounded(index, size):
    return jnp.minimum(jnp.maximum(index, 0), size - 1)


def as_column(row):
    size = row.shape[1]
    eye = ones_where(iota((size, size), 0) == iota((size, size), 1))
    return dot_nt(eye, row, precision=lax.Precision.HIGHEST)


def tile_plan(rows, cols, row_blocks):
    count = rows.shape[1]
    key = (cols * row_blocks + rows).astype(F32)
    column = as_column(jnp.broadcast_to(key, (8, count)))[:, 0:1]
    square = (count, count)
    earlier = iota(square, 1) < iota(square, 0)
    twin = (key == column) & earlier
    rank = jnp.sum(ones_where((key < column) | twin), axis=1, keepdims=True)
    chained = jnp.sum(ones_where(twin), axis=1, keepdims=True) > 0.0
    placed = rank == iota(square, 1).astype(F32)
    order = jnp.sum(jnp.where(placed, iota(square, 0).astype(F32), 0.0), axis=0, keepdims=True)
    chain = jnp.sum(ones_where(placed & chained), axis=0, keepdims=True)
    block = iota(square, 1).astype(F32)
    upto = jnp.sum(ones_where(column <= block), axis=0, keepdims=True)
    any_tile = jnp.sum(ones_where(column == block), axis=0, keepdims=True) > 0.0
    last = jnp.where(any_tile, upto, 0.0)
    return order.astype(jnp.int32), chain.astype(jnp.int32), last.astype(jnp.int32)


def spread_body(
    n, alphas, counts, rows, cols, send_rows, nodes, labels, base_in, tiles, out,
    base, held, sums, high, low, pick, pick_high, pick_low, start, fixed, truth, free, wide0, wide1, total, plan, plan_s,
    sent0, sent1, sent2, sent3, sent4, got0, got1, got2, got3, got4,
    part, parts, send_sems, recv_sems, part_send, part_recv, load_sems,
):
    channels, local = base.shape
    count, tile, _ = held.shape
    row_blocks, col_blocks = local // tile, high.shape[0] // tile
    slots, size = send_rows.shape[1:]
    halo = slots * size
    reach = slots // 2
    offsets = [value for value in range(-reach, reach + 1) if value != 0]
    me = lax.axis_index("row")
    sent, got = (sent0, sent1, sent2, sent3, sent4), (got0, got1, got2, got3, got4)

    barrier = pltpu.get_barrier_semaphore()

    def greet(k, _):
        pl.semaphore_signal(barrier, inc=1, device_id={"row": lax.rem(me + k, n)}, device_id_type=MESH)
        return 0

    lax.fori_loop(1, n, greet, 0)
    base_load = pltpu.make_async_copy(base_in, base, load_sems.at[0])
    base_load.start()
    step = count // CHUNKS
    loads = []
    for chunk in range(CHUNKS):
        some = pl.ds(chunk * step, step)
        loads.append(pltpu.make_async_copy(tiles.at[some], held.at[some], load_sems.at[2 + chunk]))
        loads[-1].start()

    def inside(offset):
        return (me + offset >= 0) & (me + offset < n)

    for slot, offset in enumerate(offsets):

        @pl.when(jnp.logical_not(inside(offset)))
        def _():
            for buffer in got:
                buffer[slot] = jnp.zeros(buffer.shape[1:], buffer.dtype)

    def copy(turn, k):
        return pltpu.make_async_remote_copy(
            src_ref=sent[turn].at[k],
            dst_ref=got[turn].at[slots - 1 - k],
            send_sem=send_sems.at[turn, k],
            recv_sem=recv_sems.at[turn, slots - 1 - k],
            device_id={"row": me + offsets[k]},
            device_id_type=MESH,
        )

    def send(turn, picked):
        for k in range(slots):
            sent[turn][k] = picked[k * size : (k + 1) * size, :].astype(sent[turn].dtype)
        for k, offset in enumerate(offsets):

            @pl.when(inside(offset))
            def _():
                copy(turn, k).start()

    def receive(turn):
        for slot, offset in enumerate(offsets):

            @pl.when(inside(offset))
            def _():
                copy(turn, slots - 1 - slot).wait_recv()

        return jnp.concatenate([got[turn][slot] for slot in range(slots)], axis=0)

    def over_columns(step):
        def one(j, _):
            step(pl.ds(pl.multiple_of(j * WIDTH, WIDTH), WIDTH))
            return 0

        lax.fori_loop(0, local // WIDTH, one, 0)

    def product(values, rows, columns):
        return dot(values, high[rows, columns]) + dot(values, low[rows, columns])

    def picked_local(values):
        return dot_nt(pick_high[:, :local], values) + dot_nt(pick_low[:, :local], values)

    def picked_halo(values):
        return dot(pick_high[:, local:], values) + dot(pick_low[:, local:], values)

    order, chain, last = tile_plan(rows[...], cols[...], row_blocks)
    plan[...] = jnp.zeros_like(plan)
    plan[0:1, :count] = order
    plan[1:2, :count] = chain
    plan[2:3, :count] = last
    plan_copy = pltpu.make_async_copy(plan, plan_s, load_sems.at[1])
    plan_copy.start()

    wanted = as_column(send_rows[0].astype(F32)).astype(jnp.int32)
    column, place = iota((size, local), 1), iota((size, local), 0)
    for k in range(slots):
        live = (column == wanted[:, k : k + 1]) & (place < counts[0, k])
        pick[k * size : (k + 1) * size, :] = ones_where(live).astype(BF)
    labelled_count = nodes.shape[1]
    node = as_column(jnp.broadcast_to(nodes[...].astype(F32), (8, labelled_count)))[:, 0:1].astype(jnp.int32)
    placed = ones_where(iota((labelled_count, local), 1) == node).astype(BF)
    pick[halo:, :] = placed
    onehot = ones_where(iota((channels, labelled_count), 0) == labels[...]).astype(BF)
    truth[...] = dot(onehot, placed)
    labelled = dot(jnp.ones((8, labelled_count), BF), placed)
    free[...] = 1.0 - labelled
    base_load.wait()
    start[...] = labelled[0:1, :] * (truth[...] - base[...])
    wide0[:, :local] = start[...].astype(BF)
    first = dot_nt(pick[:halo, :], wide0[:, :local])
    pl.semaphore_wait(barrier, n - 1)
    send(0, first)

    fixed[...] = truth[...] + free[0:1, :] * base[...]
    rest = base[...]
    base_pick = jnp.zeros((pick.shape[0], channels), F32)
    for _ in range(3):
        term = rest.astype(BF)
        rest = rest - term.astype(F32)
        base_pick = base_pick + dot_nt(pick[...], term)
    truth_pick = dot_nt(pick[...], truth[...].astype(BF))
    labelled_pick = dot_nt(pick[...], labelled.astype(BF))[:, 0:1]
    live_pick = dot_nt(pick[...], jnp.ones((8, local), BF))[:, 0:1]
    free_pick = live_pick - labelled_pick
    start_pick = labelled_pick * (truth_pick - base_pick)
    fixed_pick = truth_pick + free_pick * base_pick

    sums[0] = jnp.zeros((tile, tile), F32)
    plan_copy.wait()
    for load in loads:
        load.wait()

    def add(k, running):
        keep = jnp.full((tile, tile), plan_s[1, k], jnp.int32) > 0
        running = jnp.where(keep, running, 0.0) + held[bounded(plan_s[0, k], count)].astype(F32)
        sums[k + 1] = running
        return running

    lax.fori_loop(0, count, add, jnp.zeros((tile, tile), F32), unroll=8)

    def settle(c, _):
        for r in range(row_blocks):
            high_part, low_part = split(sums[bounded(plan_s[2, c * row_blocks + r], count + 1)])
            where = (pl.ds(pl.multiple_of(c * tile, tile), tile), pl.ds(r * tile, tile))
            high[where] = high_part
            low[where] = low_part
        return 0

    lax.fori_loop(0, col_blocks, settle, 0)
    group = (local + halo) // 3

    def pick_columns(j, _):
        columns = pl.ds(pl.multiple_of(j * group, tile), group)
        pick_high[:, columns] = dot_nt(pick[...], high[columns, :]).astype(BF)
        pick_low[:, columns] = dot_nt(pick[...], low[columns, :]).astype(BF)
        return 0

    lax.fori_loop(0, 3, pick_columns, 0)

    def folded(x):
        row = jnp.sum(x, axis=0, keepdims=True)
        return jnp.sum(row, axis=1, keepdims=True)

    weight = alphas[0]
    picked = picked_local(wide0[:, :local])
    edge = receive(0)
    picked = picked + picked_halo(edge)
    picked = (1.0 - weight) * start_pick + weight * picked
    send(1, picked)
    send(4, fixed_pick)
    wide0[:, local:] = edge.T

    def first_hop(columns):
        spread = product(wide0[...], slice(None), columns)
        wide1[:, columns] = ((1.0 - weight) * start[:, columns] + weight * spread).astype(BF)

    over_columns(first_hop)

    picked = picked_local(wide1[:, :local])
    edge = receive(1)
    picked = picked + picked_halo(edge)
    picked = (1.0 - weight) * start_pick + weight * picked
    mass, spread_mass = folded(jnp.abs(start_pick[halo:, :])), folded(jnp.abs(picked[halo:, :]))
    part[...] = jnp.where(iota((1, 128), 1) < 64, mass, spread_mass)

    def part_copy(k):
        return pltpu.make_async_remote_copy(
            src_ref=part,
            dst_ref=parts.at[k - 1],
            send_sem=part_send.at[k - 1],
            recv_sem=part_recv.at[k - 1],
            device_id={"row": lax.rem(me + k, n)},
            device_id_type=MESH,
        )

    def part_start(k, _):
        part_copy(k).start()
        return 0

    lax.fori_loop(1, n, part_start, 0)
    moving_pick = free_pick * picked
    send(2, moving_pick)
    wide1[:, local:] = edge.T

    def second_hop(columns):
        spread = product(wide1[...], slice(None), columns)
        total[:, columns] = free[0:1, columns] * ((1.0 - weight) * start[:, columns] + weight * spread)

    over_columns(second_hop)

    def part_wait(k, _):
        part_copy(k).wait_recv()
        return 0

    lax.fori_loop(1, n, part_wait, 0)
    sums_all = part[...] + jnp.sum(parts[...], axis=0)
    entries = n * labelled_count * channels
    scale = (sums_all[:, 0:1] / entries) / (sums_all[:, 64:65] / entries + 1e-06)
    start[...] = fixed[...] + scale * total[...]
    wide0[:, :local] = start[...].astype(BF)
    anchored_pick = fixed_pick + scale * moving_pick

    weight = alphas[1]
    picked = picked_local(wide0[:, :local])
    fixed_edge = receive(4)
    edge = (fixed_edge + scale * receive(2)).astype(BF)
    picked = picked + picked_halo(edge)
    send(3, truth_pick + free_pick * ((1.0 - weight) * anchored_pick + weight * picked))
    wide0[:, local:] = edge.T

    def third_hop(columns):
        spread = product(wide0[...], slice(None), columns)
        smoothed = (1.0 - weight) * start[:, columns] + weight * spread
        wide1[:, columns] = (truth[:, columns] + free[0:1, columns] * smoothed).astype(BF)

    over_columns(third_hop)

    def fourth_hop(columns):
        total[:, columns] = product(wide1[:, :local], slice(0, local), columns)

    over_columns(fourth_hop)
    wide1[:, local:] = receive(3).T

    def finish(columns):
        spread = total[:, columns] + product(wide1[:, local:], slice(local, None), columns)
        smoothed = (1.0 - weight) * start[:, columns] + weight * spread
        out[:, columns] = truth[:, columns] + free[0:1, columns] * smoothed

    over_columns(finish)

    for turn in range(len(sent)):
        for k, offset in enumerate(offsets):

            @pl.when(inside(offset))
            def _():
                copy(turn, k).wait_send()

    def part_end(k, _):
        part_copy(k).wait_send()
        return 0

    lax.fori_loop(1, n, part_end, 0)


def shards(
    alphas, base_scores, tile_values, tile_rows, tile_cols, send_rows, send_count, train_nodes, train_labels
):
    n = lax.axis_size("row")
    channels, local = base_scores.shape
    slots, size = send_rows.shape[1:]
    count, tile, _ = tile_values.shape
    halo = slots * size
    picks = halo + train_nodes.shape[0]
    vmem = pl.BlockSpec(memory_space=pltpu.VMEM)
    smem = pl.BlockSpec(memory_space=pltpu.SMEM)
    hbm = pl.BlockSpec(memory_space=pl.ANY)
    whole = pltpu.VMEM((channels, local), F32)
    wide = pltpu.VMEM((channels, local + halo), BF)
    lanes = -(-count // 128) * 128
    boundary = [pltpu.VMEM((slots, size, channels), kind) for kind in (BF, BF, F32, BF, F32)]
    return pl.pallas_call(
        functools.partial(spread_body, n),
        out_shape=pltpu.VMEM((channels, local), F32),
        in_specs=[smem, smem, vmem, vmem, vmem, vmem, vmem, hbm, hbm],
        out_specs=vmem,
        scratch_shapes=[
            whole,
            pltpu.VMEM(tile_values.shape, BF),
            pltpu.VMEM((count + 1, tile, tile), F32),
            pltpu.VMEM((local + halo, local), BF),
            pltpu.VMEM((local + halo, local), BF),
            pltpu.VMEM((picks, local), BF),
            pltpu.VMEM((picks, local + halo), BF),
            pltpu.VMEM((picks, local + halo), BF),
            whole,
            whole,
            whole,
            pltpu.VMEM((8, local), F32),
            wide,
            wide,
            whole,
            pltpu.VMEM((8, lanes), jnp.int32),
            pltpu.SMEM((8, lanes), jnp.int32),
            *boundary,
            *boundary,
            pltpu.VMEM((1, 128), F32),
            pltpu.VMEM((n - 1, 1, 128), F32),
            pltpu.SemaphoreType.DMA((5, slots)),
            pltpu.SemaphoreType.DMA((5, slots)),
            pltpu.SemaphoreType.DMA((n - 1,)),
            pltpu.SemaphoreType.DMA((n - 1,)),
            pltpu.SemaphoreType.DMA((2 + CHUNKS,)),
        ],
        compiler_params=pltpu.CompilerParams(collective_id=0, has_side_effects=True, vmem_limit_bytes=LIMIT),
        name="spread",
    )(
        alphas, send_count, tile_rows.reshape(1, -1), tile_cols.reshape(1, -1), send_rows,
        train_nodes.reshape(1, -1), train_labels.reshape(1, -1), base_scores, tile_values,
    )


def solution(mesh):
    return jax.shard_map(
        shards,
        mesh=mesh,
        in_specs=(
            P("sweep"), P(None, "row"), P("row", None, None), P("row"), P("row"),
            P("row", None, None), P("row", None), P("row"), P("row"),
        ),
        out_specs=P("sweep", "row"),
        check_vma=False,
    )
```
